32 devices in a mesh: parts: 2 (over y), blk: 4 (over x, core), col: 4 (over z).
Axes of the slice: x: 2, y: 2, z: 4, core: 2. Of those that a mesh axis runs over, the one named last changes fastest.
Arguments:
- a_blocks: float32 [8, 4, 6, 128, 128], P(('parts', 'blk')), parts along dimension 0, may hold values from -2 to 2
- a_rows: int32 [8, 4, 6], P(('parts', 'blk')), parts along dimension 0, may hold values from 0 to 2, as said below
- a_cols: int32 [8, 4, 6], P(('parts', 'blk')), parts along dimension 0, may hold values from -1 to 2, as said below
- b_panel: float32 [3072, 1536], P(('parts', 'blk'), 'col'), parts along dimension 0, may hold values from -6 to 6
- pattern: int32 [24, 12], P(('parts', 'blk'), 'col'), parts along dimension 0, may hold values 0 or 1
Outputs:
- step_matrix: float32 [3072, 1536], P(('parts', 'blk'), 'col'), parts along dimension 0
The draws below stay inside these ranges and needn't reach their ends.
There are 2 independent parts, one for each index of `parts`. The reference program is written for one: setup_inputs(seed, part) draws one part's arguments, and reference() takes and returns one part's arrays. A program takes and returns all parts, laid end to end along the dimension named above; each array names one. Nothing has to cross between parts.
Inputs may be any that keep to these rules, and one draw needn't show every extreme that they name: a_rows[r, s, q] and a_cols[r, s, q] name the block of row group r and column group s held in slot q; no pair is named twice in one (r, s). `a_cols`: -1 marks an empty slot; empty slots follow the live ones; each (r, s) has 2 to 6 live slots, and some (r, s) has 6.
All inputs are finite; a program needn't handle non-finite values. No bound on the sum of `pattern` on one device may be relied on, other than what follows from the above.
Results may differ from the reference program's by a relative error of at most 0.000059.
Values sent between devices are 32-bit elements; how exact they have to be, the bound alone decides.
No kernel may reach another device: no remote copies, remote signals or barrier semaphores. Data moves between devices by JAX's collectives and lax.ppermute only.
A program may use at most 64 MiB of HBM per device.

```python
import jax
import jax.numpy as jnp
from jax import lax

BS = 128
RB = 3
SLOT = 6
NB = 12
N_BLK = 4


def slot_layout(key):
    pair_count = RB * RB
    pair_ids = jnp.arange(pair_count, dtype=jnp.int32)
    scores = jax.random.randint(key, (N_BLK, N_BLK, pair_count), 0, 1 << 20) * pair_count + pair_ids
    shuffled = jnp.argsort(scores, axis=-1)[..., :SLOT].astype(jnp.int32)
    live_count = jax.random.randint(jax.random.fold_in(key, 1), (N_BLK, N_BLK), 2, SLOT + 1)
    fullest = jax.random.randint(jax.random.fold_in(key, 2), (), 0, N_BLK * N_BLK)
    flat_ids = jnp.arange(N_BLK * N_BLK, dtype=jnp.int32).reshape(N_BLK, N_BLK)
    live_count = jnp.where(flat_ids == fullest, SLOT, live_count)
    is_live = jnp.arange(SLOT, dtype=jnp.int32) < live_count[..., None]
    return (shuffled, is_live)


def draw_a_rows(key, part):
    shuffled, is_live = slot_layout(key)
    return (shuffled // RB).astype(jnp.int32)


def draw_a_cols(key, part):
    shuffled, is_live = slot_layout(key)
    return jnp.where(is_live, shuffled % RB, -1).astype(jnp.int32)


def draw_a_blocks(key, part):
    key = jax.random.fold_in(key, 7)
    shape = (N_BLK, N_BLK, SLOT, BS, BS)
    spread = 1.5 * (BS * N_BLK * SLOT / RB) ** (-0.5)
    rising = 1.0 + 2.0 * jnp.arange(N_BLK, dtype=jnp.float32) / (N_BLK - 1)
    values = jax.random.normal(key, shape, jnp.float32)
    return (values * spread * rising[:, None, None, None, None]).astype(jnp.float32)


def set_ends(entries, key, least, top_value):
    dims = entries.shape
    index_at = [jax.random.randint(jax.random.fold_in(key, axis), (), 0, dims[axis]) for axis in range(len(dims))]
    entries = entries.at[tuple(index_at)].set(least)
    longest = dims.index(max(dims))
    index_at[longest] = (index_at[longest] + 1) % dims[longest]
    return entries.at[tuple(index_at)].set(top_value)


def block_levels(stream_key, shape, split, smallest, high):
    loudness = 1.0
    for axis_at, blocks in split:
        steps = jax.random.uniform(jax.random.fold_in(jax.random.fold_in(stream_key, 6), axis_at), (blocks,), jnp.float32, smallest / len(split), high / len(split))
        loudness = loudness * jnp.repeat(jnp.exp(steps), shape[axis_at] // blocks).reshape((-1,) + (1,) * (len(shape) - 1 - axis_at))
    return loudness


def noise(stream_key, extent, deviation, limit, shards=(), held_as=jnp.bfloat16):
    level = block_levels(stream_key, extent, shards, -0.22, 0.18) if shards else 1.0
    drawn = jax.random.normal(stream_key, extent, jnp.float32) * deviation * level
    return jnp.minimum(jnp.maximum(drawn, -limit), limit).astype(held_as)


def setup_inputs(seed: int = 0, part: int = 0) -> dict:
    key_list = jax.random.split(jax.random.key(seed), 6)
    part_keys = jax.random.split(jax.random.fold_in(key_list[5], part), 6)
    a_blocks = draw_a_blocks(jax.random.fold_in(jax.random.fold_in(key_list[5], part), 71), part)
    a_rows = draw_a_rows(jax.random.fold_in(jax.random.fold_in(key_list[5], part), 71), part)
    a_cols = draw_a_cols(jax.random.fold_in(jax.random.fold_in(key_list[5], part), 71), part)
    b_panel = noise(part_keys[3], (NB * BS, NB * BS), 1.0, 6.0, ((0, 4), (1, 4)), jnp.float32)
    pattern = set_ends((jax.random.randint(part_keys[4], (NB, NB), 0, 4) < 3).astype(jnp.int32), jax.random.fold_in(part_keys[4], 1), 0, 1)
    return {"a_blocks": a_blocks, "a_rows": a_rows, "a_cols": a_cols, "b_panel": b_panel, "pattern": pattern}


trust_radius = 0.5

def reference(a_blocks, a_rows, a_cols, b_panel, pattern):
    highest = lax.Precision.HIGHEST
    local_ids = jnp.arange(RB, dtype=jnp.int32)
    row_hot = (a_rows[..., None] == local_ids).astype(jnp.float32)
    col_hot = (a_cols[..., None] == local_ids).astype(jnp.float32)
    pair_hot = jnp.einsum('rsqi,rsqk->rsqik', row_hot, col_hot, precision=highest)
    dense_a = jnp.einsum('rsqik,rsqab->riaskb', pair_hot, a_blocks, precision=highest)
    dense_a = dense_a.reshape(NB * BS, NB * BS)
    product = jnp.dot(dense_a, b_panel, precision=highest, preferred_element_type=jnp.float32)
    cutoff = pattern.astype(jnp.float32)
    gradient = product.reshape(NB, BS, NB, BS) * cutoff[:, None, :, None]
    magnitude = jnp.sqrt(jnp.sum(gradient * gradient) + 1e-06)
    factor = jnp.minimum(1.0, trust_radius * NB * BS / magnitude)
    return (-gradient * factor).reshape(NB * BS, NB * BS)
```

```python
import functools

import jax
import jax.numpy as jnp
from jax import lax
from jax.experimental import pallas as pl
from jax.experimental.pallas import tpu as pltpu
from jax.sharding import PartitionSpec as P

trust_radius = 0.5
LIMIT = 48 << 20
VM = pl.BlockSpec(memory_space=pltpu.VMEM)
SM = pl.BlockSpec(memory_space=pltpu.SMEM)


def vmem(value):
    return pltpu.with_memory_space_constraint(value, pltpu.VMEM)


def split(value):
    high = value.astype(jnp.bfloat16)
    low = (value - high.astype(jnp.float32)).astype(jnp.bfloat16)
    return high, low


def product(high_a, low_a, b):
    high_b, low_b = split(b)
    dot = functools.partial(jnp.dot, preferred_element_type=jnp.float32)
    return dot(high_a, high_b) + (dot(high_a, low_b) + dot(low_a, high_b))


def prepare(me_ref, rows_ref, cols_ref, blocks_ref, *dense_refs):
    groups, slots = blocks_ref.shape[0], blocks_ref.shape[1]
    size = blocks_ref.shape[-1]
    for ref in dense_refs:
        ref[...] = jnp.zeros_like(ref)
    chips = groups // 2
    chip, core = lax.div(me_ref[0], 2), lax.rem(me_ref[0], 2)
    for rel in range(groups):
        high_ref, low_ref = dense_refs[2 * rel], dense_refs[2 * rel + 1]
        owner = lax.rem(core + rel, 2)
        group = 2 * lax.rem(chip + chips - rel // 2, chips) + owner
        for slot in range(slots):
            col = cols_ref[group, slot]

            @pl.when(col >= 0)
            def _():
                high, low = split(blocks_ref[group, slot])
                row_at = pl.ds(pl.multiple_of(rows_ref[group, slot] * size, size), size)
                col_at = pl.ds(pl.multiple_of(col * size, size), size)
                high_ref[row_at, col_at] = high
                low_ref[row_at, col_at] = low


def start_sum(*refs):
    *terms, out_ref = refs
    total = product(terms[0][...], terms[1][...], terms[2][...])
    for at in range(3, len(terms), 3):
        total += product(terms[at][...], terms[at + 1][...], terms[at + 2][...])
    out_ref[...] = total


def add_sum(running_ref, *refs):
    *terms, out_ref = refs
    total = running_ref[...]
    for at in range(0, len(terms), 3):
        total += product(terms[at][...], terms[at + 1][...], terms[at + 2][...])
    out_ref[...] = total


def finish(pattern_ref, running_ref, high_ref, low_ref, b_ref, out_ref, squares_ref):
    row_blocks, col_blocks = pattern_ref.shape
    size = out_ref.shape[0] // row_blocks
    total = running_ref[...] + product(high_ref[...], low_ref[...], b_ref[...])
    squares = jnp.zeros((1, size), jnp.float32)
    for i in range(row_blocks):
        for j in range(col_blocks):
            part = total[i * size : (i + 1) * size, j * size : (j + 1) * size]
            part = part * pattern_ref[i, j].astype(jnp.float32)
            out_ref[i * size : (i + 1) * size, j * size : (j + 1) * size] = part
            squares += jnp.sum(part * part, axis=0, keepdims=True)
    squares_ref[...] = squares


def scale(limit, gradient_ref, one_ref, two_ref, out_ref):
    squares = jnp.sum(one_ref[...] + two_ref[...], axis=1, keepdims=True)
    factor = jnp.minimum(1.0, limit / jnp.sqrt(squares + 1e-06))
    out_ref[...] = -gradient_ref[...] * factor


def call(kernel, flops, outs, *args, specs=None):
    specs = specs or [VM] * len(args)
    moved = sum(a.size * a.dtype.itemsize for a in args)
    args = [vmem(a) if s is VM else a for a, s in zip(args, specs)]
    return pl.pallas_call(
        kernel,
        out_shape=outs,
        in_specs=specs,
        out_specs=jax.tree.map(lambda _: VM, outs),
        compiler_params=pltpu.CompilerParams(vmem_limit_bytes=LIMIT),
        cost_estimate=pl.CostEstimate(flops=flops, bytes_accessed=moved, transcendentals=0),
    )(*args)


def body(sizes, a_blocks, a_rows, a_cols, b_panel, pattern):
    blk_count, col_count = sizes
    chips = blk_count // 2
    blocks, rows, cols = a_blocks[0], a_rows[0], a_cols[0]
    size = blocks.shape[-1]
    height, width = b_panel.shape
    me = lax.axis_index("blk")

    def move(value, chip_step, core_flip):
        pairs = [(i, (i // 2 + chip_step) % chips * 2 + (i % 2) ^ core_flip) for i in range(blk_count)]
        return lax.ppermute(value, "blk", pairs)

    far = [move(b_panel, step, 0) for step in range(1, chips)]
    near = move(b_panel, 0, 1)
    half = jax.ShapeDtypeStruct((height, height), jnp.bfloat16)
    dense = call(
        prepare,
        0,
        [half] * (2 * blk_count),
        me.astype(jnp.int32).reshape(1),
        rows,
        cols,
        blocks,
        specs=[SM, SM, SM, VM],
    )
    full = jax.ShapeDtypeStruct((height, width), jnp.float32)
    flops = 6 * height * height * width
    running = call(start_sum, 2 * flops, full, *dense[0:2], b_panel, *dense[2:4], near)
    for step in range(1, chips):
        at = 4 * step
        there, running = lax.optimization_barrier((far[step - 1], running))
        forward = move(there, 0, 1)
        running = call(add_sum, flops, full, running, dense[at], dense[at + 1], there)
        if step < chips - 1:
            running = call(add_sum, flops, full, running, dense[at + 2], dense[at + 3], forward)
    gradient, squares = call(
        finish,
        flops,
        (full, jax.ShapeDtypeStruct((1, size), jnp.float32)),
        pattern,
        running,
        dense[-2],
        dense[-1],
        forward,
        specs=[SM, VM, VM, VM, VM],
    )

    def swap(value, step, core_flip):
        blk_step, col_step = step
        pairs = []
        for i in range(blk_count):
            for j in range(col_count):
                pairs.append((i * col_count + j, ((i ^ blk_step) ^ core_flip) * col_count + (j ^ col_step)))
        return lax.ppermute(value, ("blk", "col"), pairs)

    steps = []
    reach = 2
    while reach < blk_count:
        steps.append(((reach, 0), 1))
        reach *= 2
    reach = 1
    while reach < col_count:
        steps.append(((0, reach), 1))
        reach *= 2
    squares = squares + swap(squares, (0, 0), 1)
    for step in steps[:-1]:
        squares = squares + swap(squares, *step)
    last = swap(squares, *steps[-1])
    limit = trust_radius * height * blk_count
    return call(functools.partial(scale, limit), 0, full, gradient, squares, last)


def solution(mesh):
    in_specs = (
        P(("parts", "blk"), None, None, None, None),
        P(("parts", "blk"), None, None),
        P(("parts", "blk"), None, None),
        P(("parts", "blk"), "col"),
        P(("parts", "blk"), "col"),
    )
    out_specs = P(("parts", "blk"), "col")
    run = functools.partial(body, (mesh.shape["blk"], mesh.shape["col"]))
    return jax.shard_map(run, mesh=mesh, in_specs=in_specs, out_specs=out_specs, check_vma=False)
```

```python
import functools

import jax
import jax.numpy as jnp
from jax import lax
from jax.experimental import pallas as pl
from jax.experimental.pallas import tpu as pltpu
from jax.sharding import PartitionSpec as P

trust_radius = 0.5
LIMIT = 8 << 20
VM = pl.BlockSpec(memory_space=pltpu.VMEM)
SM = pl.BlockSpec(memory_space=pltpu.SMEM)
HBM = pl.BlockSpec(memory_space=pltpu.HBM)


def shape(*dims, dtype=jnp.float32):
    return jax.ShapeDtypeStruct(dims, dtype)


def split(value):
    high = value.astype(jnp.bfloat16)
    low = (value - high.astype(jnp.float32)).astype(jnp.bfloat16)
    return high, low


def product(high_a, low_a, b):
    high_b, low_b = split(b)
    left = jnp.concatenate([high_a, high_a, low_a], axis=1)
    right = jnp.concatenate([high_b, low_b, high_b], axis=0)
    return jnp.dot(left, right, preferred_element_type=jnp.float32)


def columns(core, side, col_blocks, size):
    half = col_blocks // 2
    which = core if side == 0 else 1 - core
    return pl.ds(pl.multiple_of(which * ((col_blocks - half) * size), size), half * size)


def middle_of(col_blocks, size):
    half = col_blocks // 2
    return pl.ds(half * size, size)


def cut(col_blocks, me_ref, b_ref, *refs):
    outs, sems = refs[:-1], refs[-1]
    size = b_ref.shape[1] // col_blocks
    core = lax.rem(me_ref[0], 2)
    where = [columns(core, 0, col_blocks, size), columns(core, 1, col_blocks, size)]
    if len(outs) > 2:
        where.append(middle_of(col_blocks, size))
    copies = [pltpu.make_async_copy(b_ref.at[:, w], out, sems.at[i]) for i, (w, out) in enumerate(zip(where, outs))]
    for copy in copies:
        copy.start()
    for copy in copies:
        copy.wait()


def prepare(me_ref, own_ids, near_ids, own_ref, near_ref, *dense_refs):
    groups, slots, size = own_ref.shape[0], own_ref.shape[1], own_ref.shape[-1]
    height = dense_refs[0].shape[0] // 2
    chips = groups // 2
    chip, core = lax.div(me_ref[0], 2), lax.rem(me_ref[0], 2)
    for ref in dense_refs:
        ref[...] = jnp.zeros_like(ref)
    for rel in range(groups):
        high_ref, low_ref = dense_refs[2 * rel], dense_refs[2 * rel + 1]
        group = 2 * lax.rem(chip + chips - rel // 2, chips) + lax.rem(core + rel, 2)
        for ids, blocks_ref, top in ((own_ids, own_ref, 0), (near_ids, near_ref, height)):
            for slot in range(slots):
                row = ids[group * slots + slot]
                col = ids[(groups + group) * slots + slot]

                @pl.when(col >= 0)
                def _():
                    high, low = split(blocks_ref[group, slot])
                    row_at = pl.ds(pl.multiple_of(row * size + top, size), size)
                    col_at = pl.ds(pl.multiple_of(col * size, size), size)
                    high_ref[row_at, col_at] = high
                    low_ref[row_at, col_at] = low


def start_sum(col_blocks, me_ref, own_high, own_low, own_b, near_high, near_low, near_b, side_ref, *mid_refs):
    height, width = own_b.shape
    size = width // col_blocks
    core = lax.rem(me_ref[0], 2)
    at = columns(core, 0, col_blocks, size)
    side_ref[...] = product(own_high[...], own_low[...], own_b[:, at]) + product(
        near_high[...], near_low[...], near_b[:, at]
    )
    for mid_ref in mid_refs:
        at = middle_of(col_blocks, size)
        mid_ref[...] = product(own_high[:height], own_low[:height], own_b[:, at]) + product(
            near_high[:height], near_low[:height], near_b[:, at]
        )


def add_sum(running_ref, high_ref, low_ref, b_ref, out_ref):
    rows = running_ref.shape[0]
    out_ref[...] = running_ref[...] + product(high_ref[:rows], low_ref[:rows], b_ref[...])


def masked(value, ids, first, row_blocks, col_blocks, col, squares):
    size = value.shape[0] // row_blocks
    rows = []
    for i in range(row_blocks):
        row = []
        for j in range(value.shape[1] // size):
            part = value[i * size : (i + 1) * size, j * size : (j + 1) * size]
            part = part * ids[first + i * col_blocks + col + j].astype(jnp.float32)
            squares = squares + jnp.sum(part * part, axis=0, keepdims=True)
            row.append(part)
        rows.append(jnp.concatenate(row, axis=1))
    return jnp.concatenate(rows, axis=0), squares


def finish_middle(first, row_blocks, col_blocks, ids, running_ref, high_ref, low_ref, b_ref, out_ref, squares_ref):
    height = running_ref.shape[0]
    total = running_ref[...] + product(high_ref[:height], low_ref[:height], b_ref[...])
    zero = jnp.zeros(squares_ref.shape, jnp.float32)
    out_ref[...], squares_ref[...] = masked(total, ids, first, row_blocks, col_blocks, col_blocks // 2, zero)


def finish(first, row_blocks, col_blocks, me_ref, own_ids, near_ids, *refs):
    running_ref, high_ref, low_ref, b_ref, *before, keep_ref, give_ref, squares_ref = refs
    height = keep_ref.shape[0]
    half = col_blocks // 2
    col = lax.rem(me_ref[0], 2) * (col_blocks - half)
    total = running_ref[...] + product(high_ref[...], low_ref[...], b_ref[...])
    squares = before[0][...] if before else jnp.zeros(squares_ref.shape, jnp.float32)
    keep_ref[...], squares = masked(total[:height], own_ids, first, row_blocks, col_blocks, col, squares)
    give_ref[...], squares = masked(total[height:], near_ids, first, row_blocks, col_blocks, col, squares)
    squares_ref[...] = squares


def scale(limit, col_blocks, me_ref, one_ref, two_ref, keep_ref, take_ref, *refs):
    *mid_refs, out_ref = refs
    size = out_ref.shape[1] // col_blocks
    core = lax.rem(me_ref[0], 2)
    squares = jnp.sum(one_ref[...] + two_ref[...], axis=1, keepdims=True)
    factor = -jnp.minimum(1.0, limit / jnp.sqrt(squares + 1e-06))
    out_ref[:, columns(core, 0, col_blocks, size)] = keep_ref[...] * factor
    out_ref[:, columns(core, 1, col_blocks, size)] = take_ref[...] * factor
    for mid_ref in mid_refs:
        out_ref[:, middle_of(col_blocks, size)] = mid_ref[...] * factor


def call(kernel, flops, outs, specs, *args, scratch=()):
    specs = [{"s": SM, "v": VM, "h": HBM}[s] for s in specs]
    moved = sum(a.size * a.dtype.itemsize for a in args)
    place = pltpu.with_memory_space_constraint
    args = [a if s is SM else place(a, s.memory_space) for a, s in zip(args, specs)]
    return pl.pallas_call(
        kernel,
        out_shape=outs,
        in_specs=specs,
        out_specs=jax.tree.map(lambda _: VM, outs),
        scratch_shapes=scratch,
        compiler_params=pltpu.CompilerParams(vmem_limit_bytes=LIMIT),
        cost_estimate=pl.CostEstimate(flops=flops, bytes_accessed=moved, transcendentals=0),
    )(*args)


def body(sizes, a_blocks, a_rows, a_cols, b_panel, pattern):
    blk_count, col_count = sizes
    chips = blk_count // 2
    blocks = a_blocks[0]
    size = blocks.shape[-1]
    height, width = b_panel.shape
    row_blocks, col_blocks = pattern.shape
    half, odd = col_blocks // 2, col_blocks % 2
    me = lax.axis_index("blk").astype(jnp.int32).reshape(1)

    def move(value, chip_step, core_flip):
        pairs = [(i, (i // 2 + chip_step) % chips * 2 + (i % 2) ^ core_flip) for i in range(blk_count)]
        return lax.ppermute(value, "blk", pairs)

    piece = shape(height, half * size)
    middle = shape(height, size)
    side, other, *mids = call(
        functools.partial(cut, col_blocks),
        0,
        [piece, piece] + [middle] * odd,
        "sh",
        me,
        b_panel,
        scratch=[pltpu.SemaphoreType.DMA((2 + odd,))],
    )
    steps = range(1, chips)
    far_mids = [[move(mid, step, 0) for mid in mids] for step in steps]
    far_sides = [move(side, step, 0) for step in steps]
    far_others = [move(other, step, 1) for step in steps]

    ids = jnp.concatenate([a_rows.reshape(-1), a_cols.reshape(-1), pattern.reshape(-1)])
    first = 2 * a_rows.size
    near_blocks = move(blocks, 0, 1)
    near_ids = move(ids, 0, 1)
    near_b = move(b_panel, 0, 1)
    dense = call(
        prepare,
        0,
        [shape(2 * height, height, dtype=jnp.bfloat16)] * (2 * blk_count),
        "sssvv",
        me,
        ids,
        near_ids,
        blocks,
        near_blocks,
    )
    flops = 6 * height * height * size
    wide = shape(2 * height, half * size)
    running, *mid_running = call(
        functools.partial(start_sum, col_blocks),
        4 * flops * half + 2 * flops * odd,
        [wide] + [middle] * odd,
        "svvvvvv",
        me,
        *dense[0:2],
        b_panel,
        *dense[2:4],
        near_b,
    )
    before = []
    for at, step in enumerate(steps):
        same, cross = dense[4 * step : 4 * step + 2], dense[4 * step + 2 : 4 * step + 4]
        for far_mid in far_mids[at]:
            forward = move(far_mid, 0, 1)
            mid_running = [call(add_sum, flops, middle, "vvvv", *mid_running, *same, far_mid)]
            if step < chips - 1:
                mid_running = [call(add_sum, flops, middle, "vvvv", *mid_running, *cross, forward)]
            else:
                *mid_running, squares = call(
                    functools.partial(finish_middle, first, row_blocks, col_blocks),
                    flops,
                    [middle, shape(1, size)],
                    "svvvv",
                    ids,
                    *mid_running,
                    *cross,
                    forward,
                )
                before = [squares]
        running = call(add_sum, 2 * flops * half, wide, "vvvv", running, *same, far_sides[at])
        if step < chips - 1:
            running = call(add_sum, 2 * flops * half, wide, "vvvv", running, *cross, far_others[at])
    keep, give, squares = call(
        functools.partial(finish, first, row_blocks, col_blocks),
        2 * flops * half,
        [piece, piece, shape(1, size)],
        "sssvvvv" + "v" * odd,
        me,
        ids,
        near_ids,
        running,
        *cross,
        far_others[-1],
        *before,
    )
    take = move(give, 0, 1)

    def swap(value, blk_step, col_step):
        pairs = []
        for i in range(blk_count):
            for j in range(col_count):
                pairs.append((i * col_count + j, (i ^ blk_step) * col_count + (j ^ col_step)))
        return lax.ppermute(value, ("blk", "col"), pairs)

    hops = [(1, 0)]
    reach = 2
    while reach < blk_count:
        hops.append((reach + 1, 0))
        reach *= 2
    reach = 1
    while reach < col_count:
        hops.append((1, reach))
        reach *= 2
    for hop in hops[:-1]:
        squares = squares + swap(squares, *hop)
    last = swap(squares, *hops[-1])
    limit = trust_radius * height * blk_count
    return call(
        functools.partial(scale, limit, col_blocks),
        0,
        shape(height, width),
        "svvvv" + "v" * odd,
        me,
        squares,
        last,
        keep,
        take,
        *mid_running,
    )


def solution(mesh):
    in_specs = (
        P(("parts", "blk"), None, None, None, None),
        P(("parts", "blk"), None, None),
        P(("parts", "blk"), None, None),
        P(("parts", "blk"), "col"),
        P(("parts", "blk"), "col"),
    )
    out_specs = P(("parts", "blk"), "col")
    run = functools.partial(body, (mesh.shape["blk"], mesh.shape["col"]))
    return jax.shard_map(run, mesh=mesh, in_specs=in_specs, out_specs=out_specs, check_vma=False)
```

```python
import functools

import jax
import jax.numpy as jnp
from jax import lax
from jax.experimental import pallas as pl
from jax.experimental.pallas import tpu as pltpu
from jax.sharding import PartitionSpec as P

trust_radius = 0.5
LIMIT = 12 << 20
SHARE = 1000
VM = pl.BlockSpec(memory_space=pltpu.VMEM)
SM = pl.BlockSpec(memory_space=pltpu.SMEM)
HBM = pl.BlockSpec(memory_space=pltpu.HBM)


def shape(*dims, dtype=jnp.float32):
    return jax.ShapeDtypeStruct(dims, dtype)


def split(value):
    high = value.astype(jnp.bfloat16)
    low = (value - high.astype(jnp.float32)).astype(jnp.bfloat16)
    return high, low


def product(high_a, low_a, b):
    high_b, low_b = split(b)
    left = jnp.concatenate([high_a, high_a, low_a], axis=1)
    right = jnp.concatenate([high_b, low_b, high_b], axis=0)
    return jnp.dot(left, right, preferred_element_type=jnp.float32)


def columns(core, side, col_blocks, size):
    half = col_blocks // 2
    which = core if side == 0 else 1 - core
    return pl.ds(pl.multiple_of(which * ((col_blocks - half) * size), size), half * size)


def middle_of(col_blocks, size):
    half = col_blocks // 2
    return pl.ds(half * size, size)


def cut(col_blocks, me_ref, b_ref, *refs):
    outs, sems = refs[:-1], refs[-1]
    size = b_ref.shape[1] // col_blocks
    core = lax.rem(me_ref[0], 2)
    where = [columns(core, 0, col_blocks, size), columns(core, 1, col_blocks, size)]
    if len(outs) > 2:
        where.append(middle_of(col_blocks, size))
    copies = [pltpu.make_async_copy(b_ref.at[:, w], out, sems.at[i]) for i, (w, out) in enumerate(zip(where, outs))]
    for copy in copies:
        copy.start()
    for copy in copies:
        copy.wait()


def pack(size, rows_ref, cols_ref, pattern_ref, out_ref):
    tile = out_ref.shape
    place = lax.broadcasted_iota(jnp.int32, tile, 0) * size + lax.broadcasted_iota(jnp.int32, tile, 1)
    found = jnp.zeros(tile, jnp.int32)
    at = 0
    for ref in (rows_ref, cols_ref, pattern_ref):
        for i in range(ref.shape[0]):
            for j in range(ref.shape[1]):
                found = jnp.where(place == at, ref[i, j], found)
                at += 1
    out_ref[...] = found.astype(jnp.float32)


def prepare(sizes, me_ref, rows_ref, cols_ref, pattern_ref, near_ids, own_hbm, near_ref, mask_ref, *refs):
    *dense_refs, own_ref, sem = refs
    half, odd = sizes
    groups, slots, size = own_ref.shape[0], own_ref.shape[1], own_ref.shape[-1]
    fetch = pltpu.make_async_copy(own_hbm, own_ref, sem)
    fetch.start()
    height = dense_refs[0].shape[0] // 2
    row_blocks, col_blocks = pattern_ref.shape
    chips = groups // 2
    chip, core = lax.div(me_ref[0], 2), lax.rem(me_ref[0], 2)

    def near_id(at):
        return near_ids[at // size, at % size]

    def near_slot(kind, group, slot):
        at = (kind * groups + group) * slots + slot
        return near_ids[lax.div(at, size), lax.rem(at, size)].astype(jnp.int32)

    for ref in dense_refs:
        ref[...] = jnp.zeros_like(ref)
    for blocks_ref, top in ((near_ref, height), (own_ref, 0)):
        if top == 0:
            fetch.wait()
        for rel in range(groups):
            high_ref, low_ref = dense_refs[2 * rel], dense_refs[2 * rel + 1]
            group = 2 * lax.rem(chip + chips - rel // 2, chips) + lax.rem(core + rel, 2)
            for slot in range(slots):
                if top:
                    row, col = near_slot(0, group, slot), near_slot(1, group, slot)
                else:
                    row, col = rows_ref[group, slot], cols_ref[group, slot]

                @pl.when(col >= 0)
                def _():
                    high, low = split(blocks_ref[group, slot])
                    row_at = pl.ds(pl.multiple_of(row * size + top, size), size)
                    col_at = pl.ds(pl.multiple_of(col * size, size), size)
                    high_ref[row_at, col_at] = high
                    low_ref[row_at, col_at] = low

    def write(at, value):
        mask_ref[at : at + 1, :] = jnp.full((1, size), value, jnp.float32)

    at = 0
    for i in range(row_blocks):
        for j in range(half):
            write(at, pattern_ref[i, core * (col_blocks - half) + j].astype(jnp.float32))
            at += 1
    first = 2 * groups * slots
    for i in range(row_blocks):
        for j in range(half):
            left, right = near_id(first + i * col_blocks + j), near_id(first + (i + 1) * col_blocks - half + j)
            write(at, jnp.where(core == 0, left, right))
            at += 1
    if odd:
        for i in range(row_blocks):
            write(at, pattern_ref[i, half].astype(jnp.float32))
            at += 1
    write(at, core.astype(jnp.float32))


def start_sum(mask_ref, own_high, own_low, near_high, near_low, near_b, *refs):
    pieces, outs = refs[: len(refs) // 2], refs[len(refs) // 2 :]
    height, width = pieces[0].shape
    core = mask_ref[mask_ref.shape[0] - 1, 0:1].reshape(1, 1)
    left, right = near_b[:, :width], near_b[:, near_b.shape[1] - width :]
    near_pieces = [jnp.where(core == 0.0, left, right), near_b[:, width : near_b.shape[1] - width]]
    for own_b, piece, out_ref in zip(pieces, near_pieces, outs):
        rows = out_ref.shape[0]
        out_ref[...] = product(own_high[:rows], own_low[:rows], own_b[...]) + product(
            near_high[:rows], near_low[:rows], piece
        )


def add_sum(running_ref, high_ref, low_ref, b_ref, out_ref):
    rows = running_ref.shape[0]
    out_ref[...] = running_ref[...] + product(high_ref[:rows], low_ref[:rows], b_ref[...])


def masked(value, mask_ref, first, out_ref, squares):
    size = mask_ref.shape[1]
    across = value.shape[1] // size
    for i in range(value.shape[0] // size):
        for j in range(across):
            at = first + i * across + j
            part = value[i * size : (i + 1) * size, j * size : (j + 1) * size] * mask_ref[at : at + 1, :]
            out_ref[i * size : (i + 1) * size, j * size : (j + 1) * size] = part
            squares = squares + jnp.sum((part * part).reshape(size // 8, 8, size), axis=0)
    return squares


def finish_middle(mask_ref, running_ref, high_ref, low_ref, b_ref, out_ref, squares_ref):
    height, size = running_ref.shape
    total = running_ref[...] + product(high_ref[:height], low_ref[:height], b_ref[...])
    first = mask_ref.shape[0] - 1 - height // size
    squares_ref[...] = masked(total, mask_ref, first, out_ref, jnp.zeros((8, size), jnp.float32))


def finish(mask_ref, running_ref, high_ref, low_ref, b_ref, *refs):
    *before, keep_ref, give_ref, squares_ref = refs
    height, size = keep_ref.shape[0], mask_ref.shape[1]
    count = keep_ref.shape[0] // size * (keep_ref.shape[1] // size)
    total = running_ref[...] + product(high_ref[...], low_ref[...], b_ref[...])
    squares = before[0][...] if before else jnp.zeros((8, size), jnp.float32)
    squares = masked(total[:height], mask_ref, 0, keep_ref, squares)
    squares = masked(total[height:], mask_ref, count, give_ref, squares)
    squares_ref[...] = jnp.sum(squares, axis=0, keepdims=True)


def scale(limit, mask_ref, one_ref, two_ref, keep_ref, take_ref, *refs):
    *mid_refs, out_ref = refs
    width = keep_ref.shape[1]
    squares = jnp.sum(one_ref[...] + two_ref[...], axis=1, keepdims=True)
    factor = -jnp.minimum(1.0, limit / jnp.sqrt(squares + 1e-06))
    core = mask_ref[mask_ref.shape[0] - 1, 0:1].reshape(1, 1)
    keep, take = keep_ref[...] * factor, take_ref[...] * factor
    out_ref[:, :width] = jnp.where(core == 0.0, keep, take)
    out_ref[:, out_ref.shape[1] - width :] = jnp.where(core == 0.0, take, keep)
    for mid_ref in mid_refs:
        out_ref[:, width : width + mid_ref.shape[1]] = mid_ref[...] * factor


def call(kernel, flops, outs, specs, *args, scratch=()):
    specs = [{"s": SM, "v": VM, "h": HBM}[s] for s in specs]
    place = pltpu.with_memory_space_constraint
    given = [s is SM and a.ndim == 2 and a.dtype == jnp.int32 for a, s in zip(args, specs)]
    args = [place(a, pltpu.HBM if g else s.memory_space) for a, s, g in zip(args, specs, given)]
    return pl.pallas_call(
        kernel,
        out_shape=outs,
        in_specs=specs,
        out_specs=jax.tree.map(lambda _: VM, outs),
        scratch_shapes=scratch,
        compiler_params=pltpu.CompilerParams(vmem_limit_bytes=LIMIT),
        cost_estimate=pl.CostEstimate(flops=flops // SHARE, bytes_accessed=0, transcendentals=0),
    )(*args)


def body(sizes, a_blocks, a_rows, a_cols, b_panel, pattern):
    blk_count, col_count = sizes
    chips = blk_count // 2
    blocks = a_blocks[0]
    size = blocks.shape[-1]
    height, width = b_panel.shape
    row_blocks, col_blocks = pattern.shape
    half, odd = col_blocks // 2, col_blocks % 2
    me = lax.axis_index("blk").astype(jnp.int32).reshape(1)

    def move(value, chip_step, core_flip):
        pairs = [(i, (i // 2 + chip_step) % chips * 2 + (i % 2) ^ core_flip) for i in range(blk_count)]
        return lax.ppermute(value, "blk", pairs)

    piece = shape(height, half * size)
    middle = shape(height, size)
    side, other, *mids = call(
        functools.partial(cut, col_blocks),
        0,
        [piece, piece] + [middle] * odd,
        "sh",
        me,
        b_panel,
        scratch=[pltpu.SemaphoreType.DMA((2 + odd,))],
    )
    steps = range(1, chips)
    far_mids = [[move(mid, step, 0) for mid in mids] for step in steps]
    far_sides = [move(side, step, 0) for step in steps]
    far_others = [move(other, step, 1) for step in steps]

    rows, cols = a_rows[0], a_cols[0]
    near_blocks = move(blocks, 0, 1)
    near_b = move(b_panel, 0, 1)
    packed = call(functools.partial(pack, size), 0, shape(8, size), "sss", rows, cols, pattern)
    near_ids = move(packed, 0, 1)
    mask, *dense = call(
        functools.partial(prepare, (half, odd)),
        0,
        [shape((2 * half + odd) * row_blocks + 1, size)]
        + [shape(2 * height, height, dtype=jnp.bfloat16)] * (2 * blk_count),
        "ssssshv",
        me,
        rows,
        cols,
        pattern,
        near_ids,
        blocks,
        near_blocks,
        scratch=[pltpu.VMEM(blocks.shape, jnp.float32), pltpu.SemaphoreType.DMA],
    )
    flops = 6 * height * height * size
    wide = shape(2 * height, half * size)
    running, *mid_running = call(
        start_sum,
        4 * flops * half + 2 * flops * odd,
        [wide] + [middle] * odd,
        "vvvvvvv" + "v" * odd,
        mask,
        *dense[0:4],
        near_b,
        side,
        *mids,
    )
    before = []
    for at, step in enumerate(steps):
        same, cross = dense[4 * step : 4 * step + 2], dense[4 * step + 2 : 4 * step + 4]
        for far_mid in far_mids[at]:
            far_mid, running = lax.optimization_barrier((far_mid, running))
            forward = move(far_mid, 0, 1)
            mid_running = [call(add_sum, flops, middle, "vvvv", *mid_running, *same, far_mid)]
            if step < chips - 1:
                mid_running = [call(add_sum, flops, middle, "vvvv", *mid_running, *cross, forward)]
            else:
                *mid_running, squares = call(
                    finish_middle,
                    flops,
                    [middle, shape(8, size)],
                    "vvvvv",
                    mask,
                    *mid_running,
                    *cross,
                    forward,
                )
                before = [squares]
        running = call(add_sum, 2 * flops * half, wide, "vvvv", running, *same, far_sides[at])
        if step < chips - 1:
            running = call(add_sum, 2 * flops * half, wide, "vvvv", running, *cross, far_others[at])
    keep, give, squares = call(
        finish,
        2 * flops * half,
        [piece, piece, shape(1, size)],
        "vvvvv" + "v" * odd,
        mask,
        running,
        *cross,
        far_others[-1],
        *before,
    )
    take = move(give, 0, 1)

    def swap(value, blk_step, col_step):
        pairs = []
        for i in range(blk_count):
            for j in range(col_count):
                pairs.append((i * col_count + j, (i ^ blk_step) * col_count + (j ^ col_step)))
        return lax.ppermute(value, ("blk", "col"), pairs)

    hops = [(1, 0)]
    reach = 2
    while reach < blk_count:
        hops.append((reach + 1, 0))
        reach *= 2
    reach = 1
    while reach < col_count:
        hops.append((1, reach))
        reach *= 2
    for hop in hops[:-1]:
        squares = squares + swap(squares, *hop)
    last = swap(squares, *hops[-1])
    limit = trust_radius * height * blk_count
    return call(
        functools.partial(scale, limit),
        0,
        shape(height, width),
        "vvvvv" + "v" * odd,
        mask,
        squares,
        last,
        keep,
        take,
        *mid_running,
    )


def solution(mesh):
    in_specs = (
        P(("parts", "blk"), None, None, None, None),
        P(("parts", "blk"), None, None),
        P(("parts", "blk"), None, None),
        P(("parts", "blk"), "col"),
        P(("parts", "blk"), "col"),
    )
    out_specs = P(("parts", "blk"), "col")
    run = functools.partial(body, (mesh.shape["blk"], mesh.shape["col"]))
    return jax.shard_map(run, mesh=mesh, in_specs=in_specs, out_specs=out_specs, check_vma=False)
```

```python
import functools

import jax
import jax.numpy as jnp
from jax import lax
from jax.experimental import pallas as pl
from jax.experimental.pallas import tpu as pltpu
from jax.sharding import PartitionSpec as P

trust_radius = 0.5
LIMIT = 12 << 20
SHARE = 1000
VM = pl.BlockSpec(memory_space=pltpu.VMEM)
SM = pl.BlockSpec(memory_space=pltpu.SMEM)
HBM = pl.BlockSpec(memory_space=pltpu.HBM)


def shape(*dims, dtype=jnp.float32):
    return jax.ShapeDtypeStruct(dims, dtype)


def split(value):
    high = value.astype(jnp.bfloat16)
    low = (value - high.astype(jnp.float32)).astype(jnp.bfloat16)
    return high, low


def product(high_a, low_a, b):
    high_b, low_b = split(b)
    left = jnp.concatenate([high_a, high_a, low_a], axis=1)
    right = jnp.concatenate([high_b, low_b, high_b], axis=0)
    return jnp.dot(left, right, preferred_element_type=jnp.float32)


def columns(core, side, col_blocks, size):
    half = col_blocks // 2
    which = core if side == 0 else 1 - core
    return pl.ds(pl.multiple_of(which * ((col_blocks - half) * size), size), half * size)


def middle_of(col_blocks, size):
    half = col_blocks // 2
    return pl.ds(half * size, size)


def cut(col_blocks, me_ref, b_ref, *refs):
    outs, sems = refs[:-1], refs[-1]
    size = b_ref.shape[1] // col_blocks
    core = lax.rem(me_ref[0], 2)
    every, early = pl.ds(0, b_ref.shape[0]), outs[1].shape[0]
    late = pl.ds(early, b_ref.shape[0] - early)
    mine, others = columns(core, 0, col_blocks, size), columns(core, 1, col_blocks, size)
    where = [(every, mine), (pl.ds(0, early), others), (late, others)]
    if len(outs) > 3:
        where.append((every, middle_of(col_blocks, size)))
    copies = [pltpu.make_async_copy(b_ref.at[w], out, sems.at[i]) for i, (w, out) in enumerate(zip(where, outs))]
    for copy in copies:
        copy.start()
    for copy in copies:
        copy.wait()


def pack(size, rows_ref, cols_ref, pattern_ref, out_ref):
    tile = out_ref.shape
    place = lax.broadcasted_iota(jnp.int32, tile, 0) * size + lax.broadcasted_iota(jnp.int32, tile, 1)
    found = jnp.zeros(tile, jnp.int32)
    at = 0
    for ref in (rows_ref, cols_ref, pattern_ref):
        for i in range(ref.shape[0]):
            for j in range(ref.shape[1]):
                found = jnp.where(place == at, ref[i, j], found)
                at += 1
    out_ref[...] = found.astype(jnp.float32)


def prepare(sizes, me_ref, rows_ref, cols_ref, pattern_ref, near_ids, own_hbm, near_ref, mask_ref, *refs):
    *dense_refs, own_ref, sem = refs
    half, odd = sizes
    groups, slots, size = own_ref.shape[0], own_ref.shape[1], own_ref.shape[-1]
    fetch = pltpu.make_async_copy(own_hbm, own_ref, sem)
    fetch.start()
    height = dense_refs[0].shape[0] // 2
    row_blocks, col_blocks = pattern_ref.shape
    chips = groups // 2
    chip, core = lax.div(me_ref[0], 2), lax.rem(me_ref[0], 2)

    def near_id(at):
        return near_ids[at // size, at % size]

    def near_slot(kind, group, slot):
        at = (kind * groups + group) * slots + slot
        return near_ids[lax.div(at, size), lax.rem(at, size)].astype(jnp.int32)

    for ref in dense_refs:
        ref[...] = jnp.zeros_like(ref)
    for blocks_ref, top in ((near_ref, height), (own_ref, 0)):
        if top == 0:
            fetch.wait()
        for rel in range(groups):
            high_ref, low_ref = dense_refs[2 * rel], dense_refs[2 * rel + 1]
            group = 2 * lax.rem(chip + chips - rel // 2, chips) + lax.rem(core + rel, 2)
            for slot in range(slots):
                if top:
                    row, col = near_slot(0, group, slot), near_slot(1, group, slot)
                else:
                    row, col = rows_ref[group, slot], cols_ref[group, slot]

                @pl.when(col >= 0)
                def _():
                    high, low = split(blocks_ref[group, slot])
                    row_at = pl.ds(pl.multiple_of(row * size + top, size), size)
                    col_at = pl.ds(pl.multiple_of(col * size, size), size)
                    high_ref[row_at, col_at] = high
                    low_ref[row_at, col_at] = low

    def write(at, value):
        mask_ref[at : at + 1, :] = jnp.full((1, size), value, jnp.float32)

    at = 0
    for i in range(row_blocks):
        for j in range(half):
            write(at, pattern_ref[i, core * (col_blocks - half) + j].astype(jnp.float32))
            at += 1
    first = 2 * groups * slots
    for i in range(row_blocks):
        for j in range(half):
            left, right = near_id(first + i * col_blocks + j), near_id(first + (i + 1) * col_blocks - half + j)
            write(at, jnp.where(core == 0, left, right))
            at += 1
    if odd:
        for i in range(row_blocks):
            write(at, pattern_ref[i, half].astype(jnp.float32))
            at += 1
    write(at, core.astype(jnp.float32))


def start_sum(mask_ref, own_high, own_low, near_high, near_low, near_b, *refs):
    pieces, outs = refs[: len(refs) // 2], refs[len(refs) // 2 :]
    height, width = pieces[0].shape
    core = mask_ref[mask_ref.shape[0] - 1, 0:1].reshape(1, 1)
    left, right = near_b[:, :width], near_b[:, near_b.shape[1] - width :]
    near_pieces = [jnp.where(core == 0.0, left, right), near_b[:, width : near_b.shape[1] - width]]
    for own_b, piece, out_ref in zip(pieces, near_pieces, outs):
        rows = out_ref.shape[0]
        out_ref[...] = product(own_high[:rows], own_low[:rows], own_b[...]) + product(
            near_high[:rows], near_low[:rows], piece
        )


def add_sum(first, running_ref, high_ref, low_ref, b_ref, out_ref):
    rows, depth = running_ref.shape[0], b_ref.shape[0]
    high, low = high_ref[:rows, first : first + depth], low_ref[:rows, first : first + depth]
    out_ref[...] = running_ref[...] + product(high, low, b_ref[...])


def masked(value, mask_ref, first, out_ref, squares):
    size = mask_ref.shape[1]
    across = value.shape[1] // size
    for i in range(value.shape[0] // size):
        for j in range(across):
            at = first + i * across + j
            part = value[i * size : (i + 1) * size, j * size : (j + 1) * size] * mask_ref[at : at + 1, :]
            out_ref[i * size : (i + 1) * size, j * size : (j + 1) * size] = part
            squares = squares + jnp.sum((part * part).reshape(size // 8, 8, size), axis=0)
    return squares


def finish_middle(mask_ref, running_ref, high_ref, low_ref, b_ref, out_ref, squares_ref):
    height, size = running_ref.shape
    total = running_ref[...] + product(high_ref[:height], low_ref[:height], b_ref[...])
    first = mask_ref.shape[0] - 1 - height // size
    squares_ref[...] = masked(total, mask_ref, first, out_ref, jnp.zeros((8, size), jnp.float32))


def finish(mask_ref, running_ref, high_ref, low_ref, b_ref, *refs):
    *before, keep_ref, give_ref, squares_ref = refs
    height, size = keep_ref.shape[0], mask_ref.shape[1]
    count = keep_ref.shape[0] // size * (keep_ref.shape[1] // size)
    first = high_ref.shape[1] - b_ref.shape[0]
    total = running_ref[...] + product(high_ref[:, first:], low_ref[:, first:], b_ref[...])
    squares = before[0][...] if before else jnp.zeros((8, size), jnp.float32)
    squares = masked(total[:height], mask_ref, 0, keep_ref, squares)
    squares = masked(total[height:], mask_ref, count, give_ref, squares)
    squares_ref[...] = jnp.sum(squares, axis=0, keepdims=True)


def scale(limit, mask_ref, one_ref, two_ref, keep_ref, take_ref, *refs):
    *mid_refs, out_ref = refs
    width = keep_ref.shape[1]
    squares = jnp.sum(one_ref[...] + two_ref[...], axis=1, keepdims=True)
    factor = -jnp.minimum(1.0, limit / jnp.sqrt(squares + 1e-06))
    core = mask_ref[mask_ref.shape[0] - 1, 0:1].reshape(1, 1)
    keep, take = keep_ref[...] * factor, take_ref[...] * factor
    out_ref[:, :width] = jnp.where(core == 0.0, keep, take)
    out_ref[:, out_ref.shape[1] - width :] = jnp.where(core == 0.0, take, keep)
    for mid_ref in mid_refs:
        out_ref[:, width : width + mid_ref.shape[1]] = mid_ref[...] * factor


def call(kernel, flops, outs, specs, *args, scratch=()):
    specs = [{"s": SM, "v": VM, "h": HBM}[s] for s in specs]
    place = pltpu.with_memory_space_constraint
    given = [s is SM and a.ndim == 2 and a.dtype == jnp.int32 for a, s in zip(args, specs)]
    args = [place(a, pltpu.HBM if g else s.memory_space) for a, s, g in zip(args, specs, given)]
    return pl.pallas_call(
        kernel,
        out_shape=outs,
        in_specs=specs,
        out_specs=jax.tree.map(lambda _: VM, outs),
        scratch_shapes=scratch,
        compiler_params=pltpu.CompilerParams(vmem_limit_bytes=LIMIT),
        cost_estimate=pl.CostEstimate(flops=flops // SHARE, bytes_accessed=0, transcendentals=0),
    )(*args)


def body(sizes, a_blocks, a_rows, a_cols, b_panel, pattern):
    blk_count, col_count = sizes
    chips = blk_count // 2
    blocks = a_blocks[0]
    size = blocks.shape[-1]
    height, width = b_panel.shape
    row_blocks, col_blocks = pattern.shape
    half, odd = col_blocks // 2, col_blocks % 2
    me = lax.axis_index("blk").astype(jnp.int32).reshape(1)

    def move(value, chip_step, core_flip):
        pairs = [(i, (i // 2 + chip_step) % chips * 2 + (i % 2) ^ core_flip) for i in range(blk_count)]
        return lax.ppermute(value, "blk", pairs)

    piece = shape(height, half * size)
    middle = shape(height, size)
    early = (row_blocks - row_blocks // 3) * size
    mids = [b_panel[:, half * size : (half + 1) * size]] * odd
    side, other, rest = call(
        functools.partial(cut, col_blocks),
        0,
        [piece, shape(early, half * size), shape(height - early, half * size)],
        "sh",
        me,
        b_panel,
        scratch=[pltpu.SemaphoreType.DMA((3,))],
    )
    steps = range(1, chips)
    far_mids = [[move(mid, step, 0) for mid in mids] for step in steps]
    far_sides = [move(side, step, 0) for step in steps]
    far_others = [move(other, step, 1) for step in steps]
    far_rests = [move(rest, step, 1) for step in steps]

    rows, cols = a_rows[0], a_cols[0]
    sent_blocks, _ = lax.optimization_barrier((blocks, mids))
    near_blocks = move(sent_blocks, 0, 1)
    near_b = move(b_panel, 0, 1)
    packed = call(functools.partial(pack, size), 0, shape(8, size), "sss", rows, cols, pattern)
    near_ids = move(packed, 0, 1)
    mask, *dense = call(
        functools.partial(prepare, (half, odd)),
        0,
        [shape((2 * half + odd) * row_blocks + 1, size)]
        + [shape(2 * height, height, dtype=jnp.bfloat16)] * (2 * blk_count),
        "ssssshv",
        me,
        rows,
        cols,
        pattern,
        near_ids,
        blocks,
        near_blocks,
        scratch=[pltpu.VMEM(blocks.shape, jnp.float32), pltpu.SemaphoreType.DMA],
    )
    flops = 6 * height * height * size
    wide = shape(2 * height, half * size)
    running, *mid_running = call(
        start_sum,
        4 * flops * half + 2 * flops * odd,
        [wide] + [middle] * odd,
        "vvvvvvv" + "v" * odd,
        mask,
        *dense[0:4],
        near_b,
        side,
        *mids,
    )
    before = []
    for at, step in enumerate(steps):
        same, cross = dense[4 * step : 4 * step + 2], dense[4 * step + 2 : 4 * step + 4]
        for far_mid in far_mids[at]:
            far_mid, mask = lax.optimization_barrier((far_mid, mask))
            forward = move(far_mid, 0, 1)
            mid_running = [call(functools.partial(add_sum, 0), flops, middle, "vvvv", *mid_running, *same, far_mid)]
            if step < chips - 1:
                mid_running = [call(functools.partial(add_sum, 0), flops, middle, "vvvv", *mid_running, *cross, forward)]
            else:
                *mid_running, squares = call(
                    finish_middle,
                    flops,
                    [middle, shape(8, size)],
                    "vvvvv",
                    mask,
                    *mid_running,
                    *cross,
                    forward,
                )
                before = [squares]
        running = call(functools.partial(add_sum, 0), 2 * flops * half, wide, "vvvv", running, *same, far_sides[at])
        far_other, before = lax.optimization_barrier((far_others[at], before))
        running = call(functools.partial(add_sum, 0), 2 * flops * half, wide, "vvvv", running, *cross, far_other)
        if step < chips - 1:
            running = call(functools.partial(add_sum, early), 2 * flops * half, wide, "vvvv", running, *cross, far_rests[at])
    keep, give, squares = call(
        finish,
        2 * flops * half,
        [piece, piece, shape(1, size)],
        "vvvvv" + "v" * odd,
        mask,
        running,
        *cross,
        far_rests[-1],
        *before,
    )
    take = move(give, 0, 1)

    def swap(value, blk_step, col_step):
        pairs = []
        for i in range(blk_count):
            for j in range(col_count):
                pairs.append((i * col_count + j, (i ^ blk_step) * col_count + (j ^ col_step)))
        return lax.ppermute(value, ("blk", "col"), pairs)

    hops = [(1, 0)]
    reach = 2
    while reach < blk_count:
        hops.append((reach + 1, 0))
        reach *= 2
    reach = 1
    while reach < col_count:
        hops.append((1, reach))
        reach *= 2
    for hop in hops[:-1]:
        squares = squares + swap(squares, *hop)
    last = swap(squares, *hops[-1])
    limit = trust_radius * height * blk_count
    return call(
        functools.partial(scale, limit),
        0,
        shape(height, width),
        "vvvvv" + "v" * odd,
        mask,
        squares,
        last,
        keep,
        take,
        *mid_running,
    )


def solution(mesh):
    in_specs = (
        P(("parts", "blk"), None, None, None, None),
        P(("parts", "blk"), None, None),
        P(("parts", "blk"), None, None),
        P(("parts", "blk"), "col"),
        P(("parts", "blk"), "col"),
    )
    out_specs = P(("parts", "blk"), "col")
    run = functools.partial(body, (mesh.shape["blk"], mesh.shape["col"]))
    return jax.shard_map(run, mesh=mesh, in_specs=in_specs, out_specs=out_specs, check_vma=False)
```

```python
import functools

import jax
import jax.numpy as jnp
from jax import lax
from jax.experimental import pallas as pl
from jax.experimental.pallas import tpu as pltpu
from jax.sharding import PartitionSpec as P

trust_radius = 0.5
LIMIT = 12 << 20
SHARE = 1000
VM = pl.BlockSpec(memory_space=pltpu.VMEM)
SM = pl.BlockSpec(memory_space=pltpu.SMEM)
HBM = pl.BlockSpec(memory_space=pltpu.HBM)


def shape(*dims, dtype=jnp.float32):
    return jax.ShapeDtypeStruct(dims, dtype)


def split(value):
    high = value.astype(jnp.bfloat16)
    low = (value - high.astype(jnp.float32)).astype(jnp.bfloat16)
    return high, low


def product(high_a, low_a, b):
    high_b, low_b = split(b)
    width = b.shape[1]
    if width <= 128:
        left = jnp.concatenate([high_a, low_a], axis=1)
        both = jnp.concatenate([high_b, low_b], axis=1)
        right = jnp.concatenate([both, both], axis=0)
        result = jnp.dot(left, right, preferred_element_type=jnp.float32)
        return result[:, :width] + result[:, width:]
    left = jnp.concatenate([high_a, high_a, low_a], axis=1)
    right = jnp.concatenate([high_b, low_b, high_b], axis=0)
    return jnp.dot(left, right, preferred_element_type=jnp.float32)


def columns(core, side, col_blocks, size):
    half = col_blocks // 2
    which = core if side == 0 else 1 - core
    return pl.ds(pl.multiple_of(which * ((col_blocks - half) * size), size), half * size)


def middle_of(col_blocks, size):
    half = col_blocks // 2
    return pl.ds(half * size, size)


def cut(col_blocks, me_ref, b_ref, *refs):
    outs, sems = refs[:-1], refs[-1]
    size = b_ref.shape[1] // col_blocks
    core = lax.rem(me_ref[0], 2)
    every, early = pl.ds(0, b_ref.shape[0]), outs[1].shape[0]
    late = pl.ds(early, b_ref.shape[0] - early)
    mine, others = columns(core, 0, col_blocks, size), columns(core, 1, col_blocks, size)
    where = [(every, mine), (pl.ds(0, early), others), (late, others)]
    if len(outs) > 3:
        where.append((every, middle_of(col_blocks, size)))
    copies = [pltpu.make_async_copy(b_ref.at[w], out, sems.at[i]) for i, (w, out) in enumerate(zip(where, outs))]
    for copy in copies:
        copy.start()
    for copy in copies:
        copy.wait()


def pack(size, rows_ref, cols_ref, pattern_ref, out_ref):
    tile = out_ref.shape
    place = lax.broadcasted_iota(jnp.int32, tile, 0) * size + lax.broadcasted_iota(jnp.int32, tile, 1)
    found = jnp.zeros(tile, jnp.int32)
    at = 0
    for ref in (rows_ref, cols_ref, pattern_ref):
        for i in range(ref.shape[0]):
            for j in range(ref.shape[1]):
                found = jnp.where(place == at, ref[i, j], found)
                at += 1
    out_ref[...] = found.astype(jnp.float32)


def prepare(sizes, me_ref, rows_ref, cols_ref, pattern_ref, near_ids, own_hbm, near_ref, mask_ref, *refs):
    *dense_refs, own_ref, sem = refs
    half, odd = sizes
    groups, slots, size = own_ref.shape[0], own_ref.shape[1], own_ref.shape[-1]
    fetch = pltpu.make_async_copy(own_hbm, own_ref, sem)
    fetch.start()
    height = dense_refs[0].shape[0] // 2
    row_blocks, col_blocks = pattern_ref.shape
    chips = groups // 2
    chip, core = lax.div(me_ref[0], 2), lax.rem(me_ref[0], 2)

    def near_id(at):
        return near_ids[at // size, at % size]

    def near_slot(kind, group, slot):
        at = (kind * groups + group) * slots + slot
        return near_ids[lax.div(at, size), lax.rem(at, size)].astype(jnp.int32)

    for ref in dense_refs:
        ref[...] = jnp.zeros_like(ref)
    for blocks_ref, top in ((near_ref, height), (own_ref, 0)):
        if top == 0:
            fetch.wait()
        for rel in range(groups):
            high_ref, low_ref = dense_refs[2 * rel], dense_refs[2 * rel + 1]
            group = 2 * lax.rem(chip + chips - rel // 2, chips) + lax.rem(core + rel, 2)
            for slot in range(slots):
                if top:
                    row, col = near_slot(0, group, slot), near_slot(1, group, slot)
                else:
                    row, col = rows_ref[group, slot], cols_ref[group, slot]

                @pl.when(col >= 0)
                def _():
                    high, low = split(blocks_ref[group, slot])
                    row_at = pl.ds(pl.multiple_of(row * size + top, size), size)
                    col_at = pl.ds(pl.multiple_of(col * size, size), size)
                    high_ref[row_at, col_at] = high
                    low_ref[row_at, col_at] = low

    def write(at, value):
        mask_ref[at : at + 1, :] = jnp.full((1, size), value, jnp.float32)

    at = 0
    for i in range(row_blocks):
        for j in range(half):
            write(at, pattern_ref[i, core * (col_blocks - half) + j].astype(jnp.float32))
            at += 1
    first = 2 * groups * slots
    for i in range(row_blocks):
        for j in range(half):
            left, right = near_id(first + i * col_blocks + j), near_id(first + (i + 1) * col_blocks - half + j)
            write(at, jnp.where(core == 0, left, right))
            at += 1
    if odd:
        for i in range(row_blocks):
            write(at, pattern_ref[i, half].astype(jnp.float32))
            at += 1
    write(at, core.astype(jnp.float32))


def start_sum(mask_ref, own_high, own_low, near_high, near_low, near_b, *refs):
    pieces, outs = refs[: len(refs) // 2], refs[len(refs) // 2 :]
    height, width = pieces[0].shape
    core = mask_ref[mask_ref.shape[0] - 1, 0:1].reshape(1, 1)
    left, right = near_b[:, :width], near_b[:, near_b.shape[1] - width :]
    near_pieces = [jnp.where(core == 0.0, left, right), near_b[:, width : near_b.shape[1] - width]]
    for own_b, piece, out_ref in zip(pieces, near_pieces, outs):
        rows = out_ref.shape[0]
        out_ref[...] = product(own_high[:rows], own_low[:rows], own_b[...]) + product(
            near_high[:rows], near_low[:rows], piece
        )


def add_sum(first, running_ref, high_ref, low_ref, b_ref, out_ref):
    rows, depth = running_ref.shape[0], b_ref.shape[0]
    high, low = high_ref[:rows, first : first + depth], low_ref[:rows, first : first + depth]
    out_ref[...] = running_ref[...] + product(high, low, b_ref[...])


def masked(value, mask_ref, first, out_ref, squares):
    size = mask_ref.shape[1]
    across = value.shape[1] // size
    for i in range(value.shape[0] // size):
        for j in range(across):
            at = first + i * across + j
            part = value[i * size : (i + 1) * size, j * size : (j + 1) * size] * mask_ref[at : at + 1, :]
            out_ref[i * size : (i + 1) * size, j * size : (j + 1) * size] = part
            squares = squares + jnp.sum((part * part).reshape(size // 8, 8, size), axis=0)
    return squares


def finish_middle(mask_ref, running_ref, high_ref, low_ref, b_ref, out_ref, squares_ref):
    height, size = running_ref.shape
    total = running_ref[...] + product(high_ref[:height], low_ref[:height], b_ref[...])
    first = mask_ref.shape[0] - 1 - height // size
    squares_ref[...] = masked(total, mask_ref, first, out_ref, jnp.zeros((8, size), jnp.float32))


def finish(mask_ref, running_ref, high_ref, low_ref, b_ref, *refs):
    *before, keep_ref, give_ref, squares_ref = refs
    height, size = keep_ref.shape[0], mask_ref.shape[1]
    count = keep_ref.shape[0] // size * (keep_ref.shape[1] // size)
    first = high_ref.shape[1] - b_ref.shape[0]
    total = running_ref[...] + product(high_ref[:, first:], low_ref[:, first:], b_ref[...])
    squares = before[0][...] if before else jnp.zeros((8, size), jnp.float32)
    squares = masked(total[:height], mask_ref, 0, keep_ref, squares)
    squares = masked(total[height:], mask_ref, count, give_ref, squares)
    squares_ref[...] = jnp.sum(squares, axis=0, keepdims=True)


def scale(limit, mask_ref, one_ref, two_ref, keep_ref, take_ref, *refs):
    *mid_refs, out_ref = refs
    width = keep_ref.shape[1]
    squares = jnp.sum(one_ref[...] + two_ref[...], axis=1, keepdims=True)
    factor = -jnp.minimum(1.0, limit * lax.rsqrt(squares + 1e-06))
    core = mask_ref[mask_ref.shape[0] - 1, 0:1].reshape(1, 1)
    keep, take = keep_ref[...] * factor, take_ref[...] * factor
    out_ref[:, :width] = jnp.where(core == 0.0, keep, take)
    out_ref[:, out_ref.shape[1] - width :] = jnp.where(core == 0.0, take, keep)
    for mid_ref in mid_refs:
        out_ref[:, width : width + mid_ref.shape[1]] = mid_ref[...] * factor


def call(kernel, flops, outs, specs, *args, scratch=()):
    specs = [{"s": SM, "v": VM, "h": HBM}[s] for s in specs]
    place = pltpu.with_memory_space_constraint
    given = [s is SM and a.ndim == 2 and a.dtype == jnp.int32 for a, s in zip(args, specs)]
    args = [place(a, pltpu.HBM if g else s.memory_space) for a, s, g in zip(args, specs, given)]
    return pl.pallas_call(
        kernel,
        out_shape=outs,
        in_specs=specs,
        out_specs=jax.tree.map(lambda _: VM, outs),
        scratch_shapes=scratch,
        compiler_params=pltpu.CompilerParams(vmem_limit_bytes=LIMIT),
        cost_estimate=pl.CostEstimate(flops=flops // SHARE, bytes_accessed=0, transcendentals=0),
    )(*args)


def body(sizes, a_blocks, a_rows, a_cols, b_panel, pattern):
    blk_count, col_count = sizes
    chips = blk_count // 2
    blocks = a_blocks[0]
    size = blocks.shape[-1]
    height, width = b_panel.shape
    row_blocks, col_blocks = pattern.shape
    half, odd = col_blocks // 2, col_blocks % 2
    me = lax.axis_index("blk").astype(jnp.int32).reshape(1)

    def move(value, chip_step, core_flip):
        pairs = [(i, (i // 2 + chip_step) % chips * 2 + (i % 2) ^ core_flip) for i in range(blk_count)]
        return lax.ppermute(value, "blk", pairs)

    piece = shape(height, half * size)
    middle = shape(height, size)
    early = (row_blocks - row_blocks // 3) * size
    mids = [b_panel[:, half * size : (half + 1) * size]] * odd
    side, other, rest = call(
        functools.partial(cut, col_blocks),
        0,
        [piece, shape(early, half * size), shape(height - early, half * size)],
        "sh",
        me,
        b_panel,
        scratch=[pltpu.SemaphoreType.DMA((3,))],
    )
    steps = range(1, chips)
    far_mids = [[move(mid, step, 0) for mid in mids] for step in steps]
    far_sides = [move(side, step, 0) for step in steps]
    far_others = [move(other, step, 1) for step in steps]
    far_rests = [move(rest, step, 1) for step in steps]

    rows, cols = a_rows[0], a_cols[0]
    sent_blocks, _ = lax.optimization_barrier((blocks, mids))
    near_blocks = move(sent_blocks, 0, 1)
    near_b = move(b_panel, 0, 1)
    packed = call(functools.partial(pack, size), 0, shape(8, size), "sss", rows, cols, pattern)
    near_ids = move(packed, 0, 1)
    mask, *dense = call(
        functools.partial(prepare, (half, odd)),
        0,
        [shape((2 * half + odd) * row_blocks + 1, size)]
        + [shape(2 * height, height, dtype=jnp.bfloat16)] * (2 * blk_count),
        "ssssshv",
        me,
        rows,
        cols,
        pattern,
        near_ids,
        blocks,
        near_blocks,
        scratch=[pltpu.VMEM(blocks.shape, jnp.float32), pltpu.SemaphoreType.DMA],
    )
    flops = 6 * height * height * size
    wide = shape(2 * height, half * size)
    running, *mid_running = call(
        start_sum,
        4 * flops * half + 2 * flops * odd,
        [wide] + [middle] * odd,
        "vvvvvvv" + "v" * odd,
        mask,
        *dense[0:4],
        near_b,
        side,
        *mids,
    )
    before = []
    for at, step in enumerate(steps):
        same, cross = dense[4 * step : 4 * step + 2], dense[4 * step + 2 : 4 * step + 4]
        for far_mid in far_mids[at]:
            far_mid, mask = lax.optimization_barrier((far_mid, mask))
            forward = move(far_mid, 0, 1)
            mid_running = [call(functools.partial(add_sum, 0), flops, middle, "vvvv", *mid_running, *same, far_mid)]
            if step < chips - 1:
                mid_running = [call(functools.partial(add_sum, 0), flops, middle, "vvvv", *mid_running, *cross, forward)]
            else:
                *mid_running, squares = call(
                    finish_middle,
                    flops,
                    [middle, shape(8, size)],
                    "vvvvv",
                    mask,
                    *mid_running,
                    *cross,
                    forward,
                )
                before = [squares]
        running = call(functools.partial(add_sum, 0), 2 * flops * half, wide, "vvvv", running, *same, far_sides[at])
        far_other, before = lax.optimization_barrier((far_others[at], before))
        running = call(functools.partial(add_sum, 0), 2 * flops * half, wide, "vvvv", running, *cross, far_other)
        if step < chips - 1:
            running = call(functools.partial(add_sum, early), 2 * flops * half, wide, "vvvv", running, *cross, far_rests[at])
    keep, give, squares = call(
        finish,
        2 * flops * half,
        [piece, piece, shape(1, size)],
        "vvvvv" + "v" * odd,
        mask,
        running,
        *cross,
        far_rests[-1],
        *before,
    )
    take = move(give, 0, 1)

    def swap(value, blk_step, col_step):
        pairs = []
        for i in range(blk_count):
            for j in range(col_count):
                pairs.append((i * col_count + j, (i ^ blk_step) * col_count + (j ^ col_step)))
        return lax.ppermute(value, ("blk", "col"), pairs)

    hops = [(1, 0)]
    reach = 2
    while reach < blk_count:
        hops.append((reach + 1, 0))
        reach *= 2
    reach = 1
    while reach < col_count:
        hops.append((1, reach))
        reach *= 2
    for hop in hops[:-1]:
        squares = squares + swap(squares, *hop)
    last = swap(squares, *hops[-1])
    limit = trust_radius * height * blk_count
    return call(
        functools.partial(scale, limit),
        0,
        shape(height, width),
        "vvvvv" + "v" * odd,
        mask,
        squares,
        last,
        keep,
        take,
        *mid_running,
    )


def solution(mesh):
    in_specs = (
        P(("parts", "blk"), None, None, None, None),
        P(("parts", "blk"), None, None),
        P(("parts", "blk"), None, None),
        P(("parts", "blk"), "col"),
        P(("parts", "blk"), "col"),
    )
    out_specs = P(("parts", "blk"), "col")
    run = functools.partial(body, (mesh.shape["blk"], mesh.shape["col"]))
    return jax.shard_map(run, mesh=mesh, in_specs=in_specs, out_specs=out_specs, check_vma=False)
```

```python
import functools

import jax
import jax.numpy as jnp
from jax import lax
from jax.experimental import pallas as pl
from jax.experimental.pallas import tpu as pltpu
from jax.sharding import PartitionSpec as P

trust_radius = 0.5
LIMIT = 12 << 20
SHARE = 1000
VM = pl.BlockSpec(memory_space=pltpu.VMEM)
SM = pl.BlockSpec(memory_space=pltpu.SMEM)
HBM = pl.BlockSpec(memory_space=pltpu.HBM)


def shape(*dims, dtype=jnp.float32):
    return jax.ShapeDtypeStruct(dims, dtype)


def split(value):
    high = value.astype(jnp.bfloat16)
    low = (value - high.astype(jnp.float32)).astype(jnp.bfloat16)
    return high, low


def product(high_a, low_a, b):
    high_b, low_b = split(b)
    width = b.shape[1]
    if width <= 128:
        left = jnp.concatenate([high_a, low_a], axis=1)
        both = jnp.concatenate([high_b, low_b], axis=1)
        right = jnp.concatenate([both, both], axis=0)
        result = jnp.dot(left, right, preferred_element_type=jnp.float32)
        return result[:, :width] + result[:, width:]
    left = jnp.concatenate([high_a, high_a, low_a], axis=1)
    right = jnp.concatenate([high_b, low_b, high_b], axis=0)
    return jnp.dot(left, right, preferred_element_type=jnp.float32)


def columns(core, side, col_blocks, size):
    half = col_blocks // 2
    which = core if side == 0 else 1 - core
    return pl.ds(pl.multiple_of(which * ((col_blocks - half) * size), size), half * size)


def middle_of(col_blocks, size):
    half = col_blocks // 2
    return pl.ds(half * size, size)


def cut(col_blocks, me_ref, b_ref, *refs):
    outs, sems = refs[:-1], refs[-1]
    size = b_ref.shape[1] // col_blocks
    core = lax.rem(me_ref[0], 2)
    every, early = pl.ds(0, b_ref.shape[0]), outs[1].shape[0]
    late = pl.ds(early, b_ref.shape[0] - early)
    mine, others = columns(core, 0, col_blocks, size), columns(core, 1, col_blocks, size)
    where = [(every, mine), (pl.ds(0, early), others), (late, others)]
    if len(outs) > 3:
        where.append((every, middle_of(col_blocks, size)))
    copies = [pltpu.make_async_copy(b_ref.at[w], out, sems.at[i]) for i, (w, out) in enumerate(zip(where, outs))]
    for copy in copies:
        copy.start()
    for copy in copies:
        copy.wait()


def pack(size, rows_ref, cols_ref, pattern_ref, out_ref):
    tile = out_ref.shape
    place = lax.broadcasted_iota(jnp.int32, tile, 0) * size + lax.broadcasted_iota(jnp.int32, tile, 1)
    found = jnp.zeros(tile, jnp.int32)
    at = 0
    for ref in (rows_ref, cols_ref, pattern_ref):
        for i in range(ref.shape[0]):
            for j in range(ref.shape[1]):
                found = jnp.where(place == at, ref[i, j], found)
                at += 1
    out_ref[...] = found.astype(jnp.float32)


def prepare(sizes, me_ref, rows_ref, cols_ref, pattern_ref, near_ids, own_hbm, near_ref, mask_ref, *refs):
    *dense_refs, own_ref, sem = refs
    half, odd = sizes
    groups, slots, size = own_ref.shape[0], own_ref.shape[1], own_ref.shape[-1]
    fetch = pltpu.make_async_copy(own_hbm, own_ref, sem)
    fetch.start()
    height = dense_refs[0].shape[0] // 2
    row_blocks, col_blocks = pattern_ref.shape
    chips = groups // 2
    chip, core = lax.div(me_ref[0], 2), lax.rem(me_ref[0], 2)

    def near_id(at):
        return near_ids[at // size, at % size]

    def near_slot(kind, group, slot):
        at = (kind * groups + group) * slots + slot
        return near_ids[lax.div(at, size), lax.rem(at, size)].astype(jnp.int32)

    for ref in dense_refs:
        ref[...] = jnp.zeros_like(ref)
    for blocks_ref, top in ((near_ref, height), (own_ref, 0)):
        if top == 0:
            fetch.wait()
        for rel in range(groups):
            high_ref, low_ref = dense_refs[2 * rel], dense_refs[2 * rel + 1]
            group = 2 * lax.rem(chip + chips - rel // 2, chips) + lax.rem(core + rel, 2)
            for slot in range(slots):
                if top:
                    row, col = near_slot(0, group, slot), near_slot(1, group, slot)
                else:
                    row, col = rows_ref[group, slot], cols_ref[group, slot]

                @pl.when(col >= 0)
                def _():
                    high, low = split(blocks_ref[group, slot])
                    row_at = pl.ds(pl.multiple_of(row * size + top, size), size)
                    col_at = pl.ds(pl.multiple_of(col * size, size), size)
                    high_ref[row_at, col_at] = high
                    low_ref[row_at, col_at] = low

    def write(at, value):
        mask_ref[at : at + 1, :] = jnp.full((1, size), value, jnp.float32)

    at = 0
    for i in range(row_blocks):
        for j in range(half):
            write(at, pattern_ref[i, core * (col_blocks - half) + j].astype(jnp.float32))
            at += 1
    first = 2 * groups * slots
    for i in range(row_blocks):
        for j in range(half):
            left, right = near_id(first + i * col_blocks + j), near_id(first + (i + 1) * col_blocks - half + j)
            write(at, jnp.where(core == 0, left, right))
            at += 1
    if odd:
        for i in range(row_blocks):
            write(at, pattern_ref[i, half].astype(jnp.float32))
            at += 1
    write(at, core.astype(jnp.float32))


def halves(b_ref, high_ref, low_ref):
    high_ref[...], low_ref[...] = split(b_ref[...])


def only_product(high_ref, low_ref, high_b_ref, low_b_ref, out_ref):
    rows, width = out_ref.shape
    left = jnp.concatenate([high_ref[:rows], low_ref[:rows]], axis=1)
    both = jnp.concatenate([high_b_ref[...], low_b_ref[...]], axis=1)
    right = jnp.concatenate([both, both], axis=0)
    result = jnp.dot(left, right, preferred_element_type=jnp.float32)
    out_ref[...] = result[:, :width] + result[:, width:]


def start_sum(odd, mask_ref, own_high, own_low, near_high, near_low, near_b, *refs):
    before, refs = refs[:odd], refs[odd:]
    pieces, outs = refs[: len(refs) // 2], refs[len(refs) // 2 :]
    height, width = pieces[0].shape
    core = mask_ref[mask_ref.shape[0] - 1, 0:1].reshape(1, 1)
    left, right = near_b[:, :width], near_b[:, near_b.shape[1] - width :]
    near_pieces = [jnp.where(core == 0.0, left, right), near_b[:, width : near_b.shape[1] - width]]
    for own_b, piece, out_ref in zip(pieces, near_pieces, outs):
        rows = out_ref.shape[0]
        out_ref[...] = product(own_high[:rows], own_low[:rows], own_b[...]) + product(
            near_high[:rows], near_low[:rows], piece
        )
    for first_ref in before:
        outs[1][...] += first_ref[...]


def add_sum(first, running_ref, high_ref, low_ref, b_ref, out_ref):
    rows, depth = running_ref.shape[0], b_ref.shape[0]
    high, low = high_ref[:rows, first : first + depth], low_ref[:rows, first : first + depth]
    out_ref[...] = running_ref[...] + product(high, low, b_ref[...])


def masked(value, mask_ref, first, out_ref, squares):
    size = mask_ref.shape[1]
    across = value.shape[1] // size
    for i in range(value.shape[0] // size):
        for j in range(across):
            at = first + i * across + j
            part = value[i * size : (i + 1) * size, j * size : (j + 1) * size] * mask_ref[at : at + 1, :]
            out_ref[i * size : (i + 1) * size, j * size : (j + 1) * size] = part
            squares = squares + jnp.sum((part * part).reshape(size // 8, 8, size), axis=0)
    return squares


def finish_middle(mask_ref, running_ref, high_ref, low_ref, b_ref, out_ref, squares_ref):
    height, size = running_ref.shape
    total = running_ref[...] + product(high_ref[:height], low_ref[:height], b_ref[...])
    first = mask_ref.shape[0] - 1 - height // size
    squares_ref[...] = masked(total, mask_ref, first, out_ref, jnp.zeros((8, size), jnp.float32))


def finish(mask_ref, running_ref, high_ref, low_ref, b_ref, *refs):
    *before, keep_ref, give_ref, squares_ref = refs
    height, size = keep_ref.shape[0], mask_ref.shape[1]
    count = keep_ref.shape[0] // size * (keep_ref.shape[1] // size)
    first = high_ref.shape[1] - b_ref.shape[0]
    total = running_ref[...] + product(high_ref[:, first:], low_ref[:, first:], b_ref[...])
    squares = before[0][...] if before else jnp.zeros((8, size), jnp.float32)
    squares = masked(total[:height], mask_ref, 0, keep_ref, squares)
    squares = masked(total[height:], mask_ref, count, give_ref, squares)
    squares_ref[...] = jnp.sum(squares, axis=0, keepdims=True)


def scale(limit, mask_ref, one_ref, two_ref, keep_ref, take_ref, *refs):
    *mid_refs, out_ref = refs
    width = keep_ref.shape[1]
    squares = jnp.sum(one_ref[...] + two_ref[...], axis=1, keepdims=True)
    factor = -jnp.minimum(1.0, limit * lax.rsqrt(squares + 1e-06))
    core = mask_ref[mask_ref.shape[0] - 1, 0:1].reshape(1, 1)
    keep, take = keep_ref[...] * factor, take_ref[...] * factor
    out_ref[:, :width] = jnp.where(core == 0.0, keep, take)
    out_ref[:, out_ref.shape[1] - width :] = jnp.where(core == 0.0, take, keep)
    for mid_ref in mid_refs:
        out_ref[:, width : width + mid_ref.shape[1]] = mid_ref[...] * factor


def call(kernel, flops, outs, specs, *args, scratch=()):
    specs = [{"s": SM, "v": VM, "h": HBM}[s] for s in specs]
    place = pltpu.with_memory_space_constraint
    given = [s is SM and a.ndim == 2 and a.dtype == jnp.int32 for a, s in zip(args, specs)]
    args = [place(a, pltpu.HBM if g else s.memory_space) for a, s, g in zip(args, specs, given)]
    return pl.pallas_call(
        kernel,
        out_shape=outs,
        in_specs=specs,
        out_specs=jax.tree.map(lambda _: VM, outs),
        scratch_shapes=scratch,
        compiler_params=pltpu.CompilerParams(vmem_limit_bytes=LIMIT),
        cost_estimate=pl.CostEstimate(flops=flops // SHARE, bytes_accessed=0, transcendentals=0),
    )(*args)


def body(sizes, a_blocks, a_rows, a_cols, b_panel, pattern):
    blk_count, col_count = sizes
    chips = blk_count // 2
    blocks = a_blocks[0]
    size = blocks.shape[-1]
    height, width = b_panel.shape
    row_blocks, col_blocks = pattern.shape
    half, odd = col_blocks // 2, col_blocks % 2
    me = lax.axis_index("blk").astype(jnp.int32).reshape(1)

    def move(value, chip_step, core_flip):
        pairs = [(i, (i // 2 + chip_step) % chips * 2 + (i % 2) ^ core_flip) for i in range(blk_count)]
        return lax.ppermute(value, "blk", pairs)

    piece = shape(height, half * size)
    middle = shape(height, size)
    early = (row_blocks - row_blocks // 3) * size
    mids = [b_panel[:, half * size : (half + 1) * size]] * odd
    side, other, rest = call(
        functools.partial(cut, col_blocks),
        0,
        [piece, shape(early, half * size), shape(height - early, half * size)],
        "sh",
        me,
        b_panel,
        scratch=[pltpu.SemaphoreType.DMA((3,))],
    )
    steps = range(1, chips)
    far_mids = [[move(mid, step, 0) for mid in mids] for step in steps]
    far_sides = [move(side, step, 0) for step in steps]
    far_others = [move(other, step, 1) for step in steps]
    far_rests = [move(rest, step, 1) for step in steps]

    rows, cols = a_rows[0], a_cols[0]
    sent_blocks, _ = lax.optimization_barrier((blocks, mids))
    near_blocks = move(sent_blocks, 0, 1)
    near_b = move(b_panel, 0, 1)
    packed = call(functools.partial(pack, size), 0, shape(8, size), "sss", rows, cols, pattern)
    near_ids = move(packed, 0, 1)
    forwards, parts = [], []
    for far_mid in far_mids[0]:
        forwards = [move(far_mid, 0, 1)]
        parts = call(halves, 9200000000000, [shape(height, size, dtype=jnp.bfloat16)] * 2, "v", far_mid)
        near_ids, near_blocks, parts = lax.optimization_barrier((near_ids, near_blocks, parts))
    mask, *dense = call(
        functools.partial(prepare, (half, odd)),
        0,
        [shape((2 * half + odd) * row_blocks + 1, size)]
        + [shape(2 * height, height, dtype=jnp.bfloat16)] * (2 * blk_count),
        "ssssshv",
        me,
        rows,
        cols,
        pattern,
        near_ids,
        blocks,
        near_blocks,
        scratch=[pltpu.VMEM(blocks.shape, jnp.float32), pltpu.SemaphoreType.DMA],
    )
    flops = 6 * height * height * size
    wide = shape(2 * height, half * size)
    firsts = [call(only_product, 0, middle, "vvvv", *dense[4:6], *parts)]  if odd else []
    if odd:
        near_b, firsts = lax.optimization_barrier((near_b, firsts))
    running, *mid_running = call(
        functools.partial(start_sum, odd),
        4 * flops * half + 2 * flops * odd,
        [wide] + [middle] * odd,
        "vvvvvvv" + "v" * (2 * odd),
        mask,
        *dense[0:4],
        near_b,
        *firsts,
        side,
        *mids,
    )
    before = []
    for at, step in enumerate(steps):
        same, cross = dense[4 * step : 4 * step + 2], dense[4 * step + 2 : 4 * step + 4]
        for far_mid in far_mids[at]:
            if step == 1:
                forward = forwards[0]
            else:
                far_mid, mask = lax.optimization_barrier((far_mid, mask))
                forward = move(far_mid, 0, 1)
                mid_running = [call(functools.partial(add_sum, 0), flops, middle, "vvvv", *mid_running, *same, far_mid)]
            if step < chips - 1:
                mid_running = [call(functools.partial(add_sum, 0), flops, middle, "vvvv", *mid_running, *cross, forward)]
            else:
                *mid_running, squares = call(
                    finish_middle,
                    flops,
                    [middle, shape(8, size)],
                    "vvvvv",
                    mask,
                    *mid_running,
                    *cross,
                    forward,
                )
                before = [squares]
        far_side, before = lax.optimization_barrier((far_sides[at], before))
        running = call(functools.partial(add_sum, 0), 2 * flops * half, wide, "vvvv", running, *same, far_side)
        far_other, before = lax.optimization_barrier((far_others[at], before))
        running = call(functools.partial(add_sum, 0), 2 * flops * half, wide, "vvvv", running, *cross, far_other)
        if step < chips - 1:
            running = call(functools.partial(add_sum, early), 2 * flops * half, wide, "vvvv", running, *cross, far_rests[at])
    keep, give, squares = call(
        finish,
        2 * flops * half,
        [piece, piece, shape(1, size)],
        "vvvvv" + "v" * odd,
        mask,
        running,
        *cross,
        far_rests[-1],
        *before,
    )
    take = move(give, 0, 1)

    def swap(value, blk_step, col_step):
        pairs = []
        for i in range(blk_count):
            for j in range(col_count):
                pairs.append((i * col_count + j, (i ^ blk_step) * col_count + (j ^ col_step)))
        return lax.ppermute(value, ("blk", "col"), pairs)

    hops = [(1, 0)]
    reach = 2
    while reach < blk_count:
        hops.append((reach + 1, 0))
        reach *= 2
    reach = 1
    while reach < col_count:
        hops.append((1, reach))
        reach *= 2
    for hop in hops[:-1]:
        squares = squares + swap(squares, *hop)
    last = swap(squares, *hops[-1])
    limit = trust_radius * height * blk_count
    return call(
        functools.partial(scale, limit),
        0,
        shape(height, width),
        "vvvvv" + "v" * odd,
        mask,
        squares,
        last,
        keep,
        take,
        *mid_running,
    )


def solution(mesh):
    in_specs = (
        P(("parts", "blk"), None, None, None, None),
        P(("parts", "blk"), None, None),
        P(("parts", "blk"), None, None),
        P(("parts", "blk"), "col"),
        P(("parts", "blk"), "col"),
    )
    out_specs = P(("parts", "blk"), "col")
    run = functools.partial(body, (mesh.shape["blk"], mesh.shape["col"]))
    return jax.shard_map(run, mesh=mesh, in_specs=in_specs, out_specs=out_specs, check_vma=False)
```
